32 devices in a mesh: rep: 4 (over z), ep: 4 (over y, x), tp: 2 (over core).
Axes of the slice: x: 2, y: 2, z: 4, core: 2. Of those that a mesh axis runs over, the one named last changes fastest.
Arguments:
- tokens: bfloat16 [2048, 3584], P(('rep', 'ep')), may hold values from -6 to 6
- cotangent: bfloat16 [2048, 3584], P(('rep', 'ep')), may hold values from -6 to 6
- routes: int32 [2048, 2], P(('rep', 'ep')), may hold values from 0 to 3, all different within a row; in each aligned block of 128 rows (0 to 127, 128 to 255, ...) at most 66 rows name the same one
- gates: float32 [2048, 2], P(('rep', 'ep')), may hold values from 0.1 to 1
- up_experts: bfloat16 [4, 3584, 2448], P('ep', 'tp'), may hold values from -0.09375 to 0.09375
- down_experts: bfloat16 [4, 2448, 3584], P('ep', None, 'tp'), may hold values from -0.125 to 0.125
- up_dense: bfloat16 [3584, 3072], P(None, 'tp'), may hold values from -0.09375 to 0.09375
- down_dense: bfloat16 [3072, 3584], P('tp'), may hold values from -0.109375 to 0.109375
Outputs:
- grad_tokens: bfloat16 [2048, 3584], P(('rep', 'ep'), 'tp')
- grad_up: bfloat16 [4, 3584, 2448], P('ep', 'tp', 'rep')
- grad_down: bfloat16 [4, 2448, 3584], P('ep', 'rep', 'tp')
The draws below stay inside these ranges and needn't reach their ends.
Inputs may be any that keep to these rules, and one draw needn't show every extreme that they name: `routes`: each row names 2 different experts. In each aligned block of 128 rows no expert is named by more than 66 rows, a bound that some block reaches.
All inputs are finite; a program needn't handle non-finite values.
Results may differ from the reference program's by a relative error of at most 0.015.
Values may be sent and summed in bfloat16 or wider, within the bound.
A program may use at most 192 MiB of HBM per device.

```python
import math
import jax
import jax.numpy as jnp
import numpy as np
from jax import lax

D = 3584
HE = 2448
HD = 3072
TOK = 128
TOP = 2
EXPERTS = 4
CAP = 66
TOKENS = 2048
N_REP = 4
N_EP = 4
N_TP = 2


def shard_levels(key, extent, pieces, least, top_value):
    loudness = 1.0
    for position, shards_of in pieces:
        draws = jax.random.uniform(jax.random.fold_in(jax.random.fold_in(key, 6), position), (shards_of,), jnp.float32, least / len(pieces), top_value / len(pieces))
        loudness = loudness * jnp.repeat(jnp.exp(draws), extent[position] // shards_of).reshape((-1,) + (1,) * (len(extent) - 1 - position))
    return loudness


def assign_block(own_key, own, number, rows, count, top, most, slope):
    ranking = jax.random.permutation(own_key, count)
    packed, ordinary = load_shares(count, rows * top, most, slope, True), load_shares(count, rows * top, most, slope, False)
    places = jnp.arange(count)

    def named(tallies, rotation):
        used = int((tallies > 0).sum())
        fixed = max(1, used // 4)
        passed = fixed + (places - fixed + rotation * (used - fixed)) % max(1, count - fixed)
        return jnp.zeros((count,), jnp.int32).at[ranking[jnp.where(places < fixed, places, passed)]].set(jnp.asarray(tallies, jnp.int32))

    tallies = jnp.where(number % 4 == 0, named(packed, number // 4), named(ordinary, number - number // 4 - 1))
    mixed = jax.random.permutation(jax.random.fold_in(own, 3), count)
    source_of, sink = mixed[0:count // 2 * 2:2], mixed[1:count // 2 * 2:2]
    room = jnp.minimum(tallies[source_of] - 1, most - tallies[sink]) // 2
    room = jnp.where((source_of == ranking[0]) | (sink == ranking[0]) | (tallies[sink] == 0), 0, jnp.maximum(room, 0))
    passed = jax.random.randint(jax.random.fold_in(own, 4), (count // 2,), 0, 1 << 20) % (room + 1)
    tallies = tallies.at[source_of].add(-passed).at[sink].add(passed)
    items = jnp.searchsorted(jnp.cumsum(tallies), jnp.arange(rows * top), side="right").astype(jnp.int32)
    listing = items.reshape(top, rows).T
    listing = listing[jax.random.permutation(jax.random.fold_in(own, 1), rows)]
    rotation = jax.random.randint(jax.random.fold_in(own, 2), (rows, 1), 0, top)
    return jnp.take_along_axis(listing, (jnp.arange(top)[None, :] + rotation) % top, axis=1)


def load_shares(count, total, limit, skew, full):
    portions = [(1 << 20) // math.isqrt(rank ** skew) + 1 for rank in range(1, count + 1)]
    largest = limit if full else min(limit, max(-(-total // count), total * portions[0] // sum(portions)))
    least = 1 if total - largest >= count - 1 else 0
    holding, surplus = [largest] + [least] * (count - 1), total - largest - least * (count - 1)
    while surplus > 0:
        movable = [i for i in range(1, count) if holding[i] < largest] or [i for i in range(1, count) if holding[i] < limit]
        pool, budget = sum([portions[i] for i in movable]), surplus
        for i in movable:
            addition = min(limit - holding[i], max(1, budget * portions[i] // pool), surplus)
            holding[i] = holding[i] + addition
            surplus = surplus - addition
    return np.array(holding)


def noise(key, shape, scale, limit, pieces=(), kind=jnp.bfloat16):
    entries = jax.random.normal(key, shape, jnp.float32) * scale
    if len(pieces) > 0:
        entries = shard_levels(key, shape, pieces, -0.22, 0.18) * entries
    return jnp.clip(entries, min=-limit, max=limit).astype(kind)


def setup_inputs(seed: int = 0) -> dict:
    key_list = jax.random.split(jax.random.key(seed), 9)
    tokens = noise(key_list[0], (TOKENS, D), 1.0, 6.0, ((0, 16),))
    cotangent = noise(key_list[1], (TOKENS, D), 1.0, 6.0, ((0, 16),))
    routes_keys = jax.random.split(jax.random.fold_in(key_list[2], 1), TOKENS // TOK)
    routes_turns = jax.random.permutation(jax.random.fold_in(key_list[2], 3), TOKENS // TOK)
    routes = jax.vmap(lambda own, number: assign_block(jax.random.fold_in(key_list[2], 2), own, number, TOK, EXPERTS, TOP, CAP, 2))(routes_keys, routes_turns).reshape((TOKENS, TOP))
    gates = jnp.clip(0.1 + 0.9 * jax.random.uniform(key_list[3], (TOKENS, TOP), jnp.float32) ** shard_levels(key_list[3], (TOKENS, TOP), ((0, 16),), -0.2, 0.2), 0.1, 1.0)
    up_experts = noise(key_list[4], (EXPERTS, D, HE), D ** -0.5, 0.09375, ((0, 4), (1, 2)))
    down_experts = noise(key_list[5], (EXPERTS, HE, D), HE ** -0.5, 0.125, ((0, 4), (2, 2)))
    up_dense = noise(key_list[6], (D, HD), D ** -0.5, 0.09375, ((1, 2),))
    down_dense = noise(key_list[7], (HD, D), HD ** -0.5, 0.109375, ((0, 2),))
    return dict(tokens=tokens, cotangent=cotangent, routes=routes, gates=gates, up_experts=up_experts, down_experts=down_experts, up_dense=up_dense, down_dense=down_dense)


def silu_grad(argument):
    sigmoid_value = jax.nn.sigmoid(argument)
    return sigmoid_value * (1.0 + argument * (1.0 - sigmoid_value))

def rounded(argument):
    return lax.optimization_barrier(argument.astype(jnp.bfloat16)).astype(jnp.float32)

def slot_table(route_block, experts):
    route_ids = route_block.reshape(-1)
    onehot = (route_ids[:, None] == jnp.arange(experts, dtype=jnp.int32)[None, :]).astype(jnp.int32)
    before = jnp.cumsum(onehot, axis=0) - onehot
    return (route_ids, lax.optimization_barrier(jnp.sum(before * onehot, axis=1)).astype(jnp.int32))

def dispatch(operands):
    x_block, dy_block, route_block, gate_block = operands
    route_ids, slot_ids = slot_table(route_block, EXPERTS)
    rows_x = jnp.broadcast_to(x_block[:, None, :], (TOK, TOP, D)).reshape(TOK * TOP, D)
    rows_g = (gate_block[:, :, None] * dy_block[:, None, :].astype(jnp.float32)).astype(jnp.bfloat16).reshape(TOK * TOP, D)
    empty_buffer = jnp.zeros((EXPERTS, CAP, D), jnp.bfloat16)
    return (empty_buffer.at[route_ids, slot_ids].set(rows_x), empty_buffer.at[route_ids, slot_ids].set(rows_g))

def expert_work(operands):
    rows_x, rows_g, w_up, w_down = operands
    local_width = D // N_TP
    row_count = rows_x.shape[0]
    hidden = jnp.zeros((row_count, HE), jnp.float32)
    grad_hidden = jnp.zeros((row_count, HE), jnp.float32)
    for part_index in range(N_TP):
        start = part_index * local_width
        hidden = hidden + rounded(jnp.dot(rows_x[:, start:start + local_width], w_up[start:start + local_width], preferred_element_type=jnp.float32))
        grad_hidden = grad_hidden + rounded(jnp.dot(rows_g[:, start:start + local_width], w_down[:, start:start + local_width].T, preferred_element_type=jnp.float32))
    activation = jax.nn.silu(hidden).astype(jnp.bfloat16)
    grad_pre = (grad_hidden * silu_grad(hidden)).astype(jnp.bfloat16)
    term_up = jnp.dot(rows_x.T, grad_pre, preferred_element_type=jnp.float32)
    term_down = jnp.dot(activation.T, rows_g, preferred_element_type=jnp.float32)
    route_grad = jnp.dot(grad_pre, w_up.T, preferred_element_type=jnp.float32).astype(jnp.bfloat16)
    return (term_up, term_down, route_grad)

def owner_rows(sent):
    return sent.reshape(N_REP, N_EP, EXPERTS, CAP, D).transpose(0, 2, 1, 3, 4).reshape(N_REP, EXPERTS, N_EP * CAP, D)

def reference(tokens, cotangent, routes, gates, up_experts, down_experts, up_dense, down_dense):
    groups = N_REP * N_EP
    x_groups = tokens.reshape(groups, TOK, D)
    dy_groups = cotangent.reshape(groups, TOK, D)
    route_groups = routes.reshape(groups, TOK, TOP)
    gate_groups = gates.reshape(groups, TOK, TOP)
    send_x, send_g = lax.map(dispatch, (x_groups, dy_groups, route_groups, gate_groups))
    recv_x = owner_rows(send_x)
    recv_g = owner_rows(send_g)

    def replica_step(totals, operands):
        rows_x, rows_g = operands
        term_up, term_down, route_grad = lax.map(expert_work, (rows_x, rows_g, up_experts, down_experts))
        return ((totals[0] + rounded(term_up), totals[1] + rounded(term_down)), route_grad)
    initial = (jnp.zeros((EXPERTS, D, HE), jnp.float32), jnp.zeros((EXPERTS, HE, D), jnp.float32))
    (up_total, down_total), route_grads = lax.scan(replica_step, initial, (recv_x, recv_g))
    returned = route_grads.reshape(N_REP, EXPERTS, N_EP, CAP, D).transpose(0, 2, 1, 3, 4).reshape(groups, EXPERTS, CAP, D)

    def combine(operands):
        returned_rows, route_block = operands
        route_ids, slot_ids = slot_table(route_block, EXPERTS)
        picked = returned_rows[route_ids, slot_ids].astype(jnp.float32)
        return picked.reshape(TOK, TOP, D).sum(axis=1)
    expert_grad = lax.map(combine, (returned, route_groups)).reshape(groups * TOK, D)
    dense_pre = jnp.dot(tokens, up_dense, preferred_element_type=jnp.float32)
    dense_back = jnp.dot(cotangent, down_dense.T, preferred_element_type=jnp.float32)
    dense_grad_pre = (dense_back * silu_grad(dense_pre)).astype(jnp.bfloat16)
    block_width = HD // N_TP
    dense_grad = jnp.zeros((groups * TOK, D), jnp.float32)
    for part_index in range(N_TP):
        start = part_index * block_width
        dense_grad = dense_grad + rounded(jnp.dot(dense_grad_pre[:, start:start + block_width], up_dense[:, start:start + block_width].T, preferred_element_type=jnp.float32))
    grad_tokens = (dense_grad + expert_grad).astype(jnp.bfloat16)
    return (grad_tokens, (up_total / N_REP).astype(jnp.bfloat16), (down_total / N_REP).astype(jnp.bfloat16))
```

```python
import jax
import jax.numpy as jnp
from jax import lax
from jax.sharding import PartitionSpec as P


def silu_grad(argument):
    sigmoid_value = jax.nn.sigmoid(argument)
    return sigmoid_value * (1.0 + argument * (1.0 - sigmoid_value))


def contract(left_operand, right_operand, left_axis, right_axis):
    return lax.dot_general(
        left_operand,
        right_operand,
        (((left_axis,), (right_axis,)), ((), ())),
        preferred_element_type=jnp.float32,
    )


def shift(value, axis, step):
    size = lax.axis_size(axis)
    return lax.ppermute(value, axis, [(i, (i + step) % size) for i in range(size)])


def dispatch_table(routes, gates, expert, capacity):
    rows = routes.shape[0]
    named = routes == expert
    member = jnp.any(named, axis=1).astype(jnp.float32)
    gate = jnp.sum(jnp.where(named, gates, 0.0), axis=1)
    token = lax.broadcasted_iota(jnp.int32, (rows, rows), 0)
    other = lax.broadcasted_iota(jnp.int32, (rows, rows), 1)
    before = jnp.sum(jnp.where(token < other, member[:, None], 0.0), axis=0).astype(jnp.int32)
    slot = lax.broadcasted_iota(jnp.int32, (capacity, rows), 0)
    hit = (slot == before[None, :]) & (member[None, :] > 0)
    slot_gate = jnp.sum(jnp.where(hit, gate[None, :], 0.0), axis=1)
    return hit.astype(jnp.bfloat16), slot_gate


def dispatched(table, slot_gate, pair):
    width = pair.shape[1] // 2
    rows = jnp.dot(table, pair, preferred_element_type=jnp.float32)
    rows_x = rows[:, :width].astype(jnp.bfloat16)
    rows_g = (slot_gate[:, None] * rows[:, width:]).astype(jnp.bfloat16)
    return jnp.concatenate([rows_x, rows_g], axis=1)


def tp_total(part):
    if lax.axis_size("tp") == 2:
        return part.astype(jnp.float32) + shift(part, "tp", 1).astype(jnp.float32)
    share = lax.psum_scatter(part, "tp", scatter_dimension=1, tiled=True)
    return lax.all_gather(share, "tp", axis=1, tiled=True).astype(jnp.float32)


def shards(tokens, cotangent, routes, gates, up_experts, down_experts, up_dense, down_dense):
    tok_rows = tokens.shape[0]
    ep_size = lax.axis_size("ep")
    rep_size = lax.axis_size("rep")
    tp_size = lax.axis_size("tp")
    ep_index = lax.axis_index("ep")
    rep_index = lax.axis_index("rep")
    tp_index = lax.axis_index("tp")
    width = up_experts.shape[1]
    hidden_units = up_experts.shape[2]
    block = hidden_units // rep_size
    capacity = min(tok_rows, 2 * tok_rows // ep_size + tok_rows // 64)
    w_up = up_experts[0]
    w_down = down_experts[0]

    offset = tp_index * width
    pair = jnp.concatenate(
        [
            lax.dynamic_slice_in_dim(tokens, offset, width, 1),
            lax.dynamic_slice_in_dim(cotangent, offset, width, 1),
        ],
        axis=1,
    )
    facts = jnp.concatenate([routes.astype(jnp.float32), gates], axis=1)
    top_count = routes.shape[1]

    shard_rows = []
    own_tables = None
    for step in range(rep_size):
        if step > 0:
            pair = shift(pair, "rep", 1)
            facts = shift(facts, "rep", 1)
        step_routes = facts[:, :top_count].astype(jnp.int32)
        step_gates = facts[:, top_count:]
        tables, pieces = [], []
        for turn in range(ep_size):
            expert = lax.rem(ep_index + turn, ep_size)
            table, slot_gate = dispatch_table(step_routes, step_gates, expert, capacity)
            tables.append(table)
            piece = dispatched(table, slot_gate, pair)
            pieces.append(shift(piece, "ep", turn) if turn else piece)
        if step == 0:
            own_tables = tables
        shard_rows.append(jnp.concatenate(pieces, axis=0))

    own = shard_rows[0]
    owner_x, owner_g = own[:, :width], own[:, width:]
    up_part = jnp.dot(owner_x, w_up, preferred_element_type=jnp.float32).astype(jnp.bfloat16)
    down_part = contract(owner_g, w_down, 1, 1).astype(jnp.bfloat16)
    hidden = tp_total(up_part)
    grad_hidden = tp_total(down_part)
    activation = jax.nn.silu(hidden).astype(jnp.bfloat16)
    grad_pre = (grad_hidden * silu_grad(hidden)).astype(jnp.bfloat16)
    route_grad = contract(grad_pre, w_up, 1, 1).astype(jnp.bfloat16)
    returned = []
    for turn in range(ep_size):
        rows = route_grad[turn * capacity:(turn + 1) * capacity]
        returned.append(shift(rows, "ep", ep_size - turn) if turn else rows)

    row_count = grad_pre.shape[0]

    def exchange(value):
        blocks = value.reshape(row_count, rep_size, block).transpose(1, 0, 2)
        taken = []
        for step in range(rep_size):
            target = lax.rem(rep_index + step, rep_size)
            part = lax.dynamic_index_in_dim(blocks, target, 0, keepdims=False)
            taken.append(shift(part, "rep", step) if step else part)
        return jnp.concatenate(taken, axis=0)

    if tp_size == 2:
        mine = exchange(jnp.where(tp_index == 0, grad_pre, activation))
        theirs = shift(mine, "tp", 1)
        all_pre = jnp.where(tp_index == 0, mine, theirs)
        all_act = jnp.where(tp_index == 0, theirs, mine)
    else:
        all_pre, all_act = exchange(grad_pre), exchange(activation)

    rows_all = jnp.concatenate(shard_rows, axis=0)
    replicas = float(rep_size)
    grad_up = (contract(rows_all[:, :width], all_pre, 0, 0) / replicas).astype(jnp.bfloat16)[None]
    grad_down = (contract(all_act, rows_all[:, width:], 0, 0) / replicas).astype(jnp.bfloat16)[None]

    dense_pre = jnp.dot(tokens, up_dense, preferred_element_type=jnp.float32)
    dense_back = contract(cotangent, down_dense, 1, 1)
    dense_grad_pre = (dense_back * silu_grad(dense_pre)).astype(jnp.bfloat16)
    dense_part = contract(dense_grad_pre, up_dense, 1, 1).astype(jnp.bfloat16)
    if tp_size == 2:
        kept = lax.dynamic_slice_in_dim(dense_part, offset, width, 1)
        passed = lax.dynamic_slice_in_dim(dense_part, (1 - tp_index) * width, width, 1)
        dense_grad = kept.astype(jnp.float32) + shift(passed, "tp", 1).astype(jnp.float32)
    else:
        dense_grad = lax.psum_scatter(
            dense_part, "tp", scatter_dimension=1, tiled=True
        ).astype(jnp.float32)

    expert_grad = contract(
        jnp.concatenate(own_tables, axis=0), jnp.concatenate(returned, axis=0), 0, 0
    )
    grad_tokens = (dense_grad + expert_grad).astype(jnp.bfloat16)
    return (grad_tokens, grad_up, grad_down)


def solution(mesh):
    in_specs = (
        P(("rep", "ep"), None),
        P(("rep", "ep"), None),
        P(("rep", "ep"), None),
        P(("rep", "ep"), None),
        P("ep", "tp", None),
        P("ep", None, "tp"),
        P(None, "tp"),
        P("tp", None),
    )
    out_specs = (P(("rep", "ep"), "tp"), P("ep", "tp", "rep"), P("ep", "rep", "tp"))
    return jax.shard_map(shards, mesh=mesh, in_specs=in_specs, out_specs=out_specs, check_vma=False)
```

```python
import jax
import jax.numpy as jnp
from jax import lax
from jax.sharding import PartitionSpec as P


def silu_grad(argument):
    sigmoid_value = jax.nn.sigmoid(argument)
    return sigmoid_value * (1.0 + argument * (1.0 - sigmoid_value))


def contract(left_operand, right_operand, left_axis, right_axis):
    return lax.dot_general(
        left_operand,
        right_operand,
        (((left_axis,), (right_axis,)), ((), ())),
        preferred_element_type=jnp.float32,
    )


def shift(value, axis, step):
    size = lax.axis_size(axis)
    return lax.ppermute(value, axis, [(i, (i + step) % size) for i in range(size)])


def dispatch_table(routes, gates, expert, capacity):
    rows = routes.shape[0]
    named = routes == expert
    member = jnp.any(named, axis=1).astype(jnp.float32)
    gate = jnp.sum(jnp.where(named, gates, 0.0), axis=1)
    token = lax.broadcasted_iota(jnp.int32, (rows, rows), 0)
    other = lax.broadcasted_iota(jnp.int32, (rows, rows), 1)
    before = jnp.sum(jnp.where(token < other, member[:, None], 0.0), axis=0).astype(jnp.int32)
    slot = lax.broadcasted_iota(jnp.int32, (capacity, rows), 0)
    hit = (slot == before[None, :]) & (member[None, :] > 0)
    slot_gate = jnp.sum(jnp.where(hit, gate[None, :], 0.0), axis=1)
    return hit.astype(jnp.bfloat16), slot_gate


def dispatched(table, slot_gate, pair):
    width = pair.shape[1] // 2
    rows = jnp.dot(table, pair, preferred_element_type=jnp.float32)
    rows_x = rows[:, :width].astype(jnp.bfloat16)
    rows_g = (slot_gate[:, None] * rows[:, width:]).astype(jnp.bfloat16)
    return jnp.concatenate([rows_x, rows_g], axis=1)


def tp_total(part):
    if lax.axis_size("tp") == 2:
        return part.astype(jnp.float32) + shift(part, "tp", 1).astype(jnp.float32)
    share = lax.psum_scatter(part, "tp", scatter_dimension=1, tiled=True)
    return lax.all_gather(share, "tp", axis=1, tiled=True).astype(jnp.float32)


def shards(tokens, cotangent, routes, gates, up_experts, down_experts, up_dense, down_dense):
    tok_rows = tokens.shape[0]
    ep_size = lax.axis_size("ep")
    rep_size = lax.axis_size("rep")
    tp_size = lax.axis_size("tp")
    ep_index = lax.axis_index("ep")
    rep_index = lax.axis_index("rep")
    tp_index = lax.axis_index("tp")
    width = up_experts.shape[1]
    hidden_units = up_experts.shape[2]
    block = hidden_units // rep_size
    capacity = min(tok_rows, 2 * tok_rows // ep_size + tok_rows // 64)
    w_up = up_experts[0]
    w_down = down_experts[0]

    slots = -(-capacity // 8) * 8
    offset = tp_index * width
    pair = jnp.concatenate(
        [
            lax.dynamic_slice_in_dim(tokens, offset, width, 1),
            lax.dynamic_slice_in_dim(cotangent, offset, width, 1),
        ],
        axis=1,
    )
    top_count = routes.shape[1]
    facts = lax.all_gather(
        jnp.concatenate([routes.astype(jnp.float32), gates], axis=1), "rep", axis=0, tiled=False
    )

    def send_rows(pair, step_routes, step_gates):
        tables, pieces = [], []
        for turn in range(ep_size):
            expert = lax.rem(ep_index + turn, ep_size)
            table, slot_gate = dispatch_table(step_routes, step_gates, expert, slots)
            tables.append(table)
            piece = dispatched(table, slot_gate, pair)
            pieces.append(shift(piece, "ep", turn) if turn else piece)
        return tables, pieces

    state = {}

    def dense_branch():
        dense_pre = jnp.dot(tokens, up_dense, preferred_element_type=jnp.float32)
        dense_back = contract(cotangent, down_dense, 1, 1)
        dense_grad_pre = (dense_back * silu_grad(dense_pre)).astype(jnp.bfloat16)
        state["dense_part"] = contract(dense_grad_pre, up_dense, 1, 1).astype(jnp.bfloat16)

    def expert_parts():
        own = jnp.concatenate(state["own"], axis=0)
        state["up_part"] = jnp.dot(
            own[:, :width], state["w_up"], preferred_element_type=jnp.float32
        ).astype(jnp.bfloat16)
        state["down_part"] = contract(own[:, width:], state["w_down"], 1, 1).astype(jnp.bfloat16)

    def expert_back():
        hidden = tp_total(state["up_part"])
        grad_hidden = tp_total(state["down_part"])
        state["act"] = jax.nn.silu(hidden).astype(jnp.bfloat16)
        state["pre"] = (grad_hidden * silu_grad(hidden)).astype(jnp.bfloat16)
        state["route_grad"] = contract(state["pre"], state["w_up"], 1, 1).astype(jnp.bfloat16)

    work = [dense_branch, expert_parts, expert_back]
    state["w_up"], state["w_down"] = w_up, w_down

    shard_rows = []
    own_tables, own_rows = send_rows(pair, routes, gates)
    shard_rows.append(own_rows)
    state["own"] = own_rows
    for step in range(1, rep_size):
        arrived = shift(pair, "rep", 1)
        if step <= len(work):
            work[step - 1]()
            held = {key: value for key, value in state.items() if key != "own"}
            arrived, held = lax.optimization_barrier((arrived, held))
            state.update(held)
        pair = arrived
        step_facts = lax.dynamic_index_in_dim(
            facts, lax.rem(rep_index - step + rep_size, rep_size), 0, keepdims=False
        )
        _, rows = send_rows(
            pair, step_facts[:, :top_count].astype(jnp.int32), step_facts[:, top_count:]
        )
        shard_rows.append(rows)
    for item in work[max(rep_size - 1, 0):]:
        item()

    grad_pre, activation, route_grad = state["pre"], state["act"], state["route_grad"]
    dense_part = state["dense_part"]
    returned = []
    for turn in range(ep_size):
        rows = route_grad[turn * slots:(turn + 1) * slots]
        returned.append(shift(rows, "ep", ep_size - turn) if turn else rows)

    row_count = grad_pre.shape[0]

    def exchange(value):
        blocks = value.reshape(row_count, rep_size, block).transpose(1, 0, 2)
        taken = []
        for step in range(rep_size):
            target = lax.rem(rep_index + step, rep_size)
            part = lax.dynamic_index_in_dim(blocks, target, 0, keepdims=False)
            taken.append(shift(part, "rep", step) if step else part)
        return jnp.concatenate(taken, axis=0)

    if tp_size == 2:
        mine = exchange(jnp.where(tp_index == 0, grad_pre, activation))
        theirs = shift(mine, "tp", 1)
        all_pre = jnp.where(tp_index == 0, mine, theirs)
        all_act = jnp.where(tp_index == 0, theirs, mine)
    else:
        all_pre, all_act = exchange(grad_pre), exchange(activation)

    early = [piece for rows in shard_rows[:-1] for piece in rows]
    replicas = float(rep_size)
    cut = len(early) * slots
    early_pre, early_act = all_pre[:cut], all_act[:cut]
    last = jnp.concatenate(shard_rows[-1], axis=0)
    up_total = contract(last[:, :width], all_pre[cut:], 0, 0)
    down_total = contract(all_act[cut:], last[:, width:], 0, 0)
    if early:
        rows_early = jnp.concatenate(early, axis=0)
        up_total += contract(rows_early[:, :width], early_pre, 0, 0)
        down_total += contract(early_act, rows_early[:, width:], 0, 0)
    grad_up = (up_total / replicas).astype(jnp.bfloat16)[None]
    grad_down = (down_total / replicas).astype(jnp.bfloat16)[None]

    if tp_size == 2:
        kept = lax.dynamic_slice_in_dim(dense_part, offset, width, 1)
        passed = lax.dynamic_slice_in_dim(dense_part, (1 - tp_index) * width, width, 1)
        dense_grad = kept.astype(jnp.float32) + shift(passed, "tp", 1).astype(jnp.float32)
    else:
        dense_grad = lax.psum_scatter(
            dense_part, "tp", scatter_dimension=1, tiled=True
        ).astype(jnp.float32)

    expert_grad = contract(
        jnp.concatenate(own_tables, axis=0), jnp.concatenate(returned, axis=0), 0, 0
    )
    grad_tokens = (dense_grad + expert_grad).astype(jnp.bfloat16)
    return (grad_tokens, grad_up, grad_down)


def solution(mesh):
    in_specs = (
        P(("rep", "ep"), None),
        P(("rep", "ep"), None),
        P(("rep", "ep"), None),
        P(("rep", "ep"), None),
        P("ep", "tp", None),
        P("ep", None, "tp"),
        P(None, "tp"),
        P("tp", None),
    )
    out_specs = (P(("rep", "ep"), "tp"), P("ep", "tp", "rep"), P("ep", "rep", "tp"))
    return jax.shard_map(shards, mesh=mesh, in_specs=in_specs, out_specs=out_specs, check_vma=False)
```

```python
import jax
import jax.numpy as jnp
from jax import lax
from jax.sharding import PartitionSpec as P


def silu_grad(argument):
    sigmoid_value = jax.nn.sigmoid(argument)
    return sigmoid_value * (1.0 + argument * (1.0 - sigmoid_value))


def contract(left_operand, right_operand, left_axis, right_axis):
    return lax.dot_general(
        left_operand,
        right_operand,
        (((left_axis,), (right_axis,)), ((), ())),
        preferred_element_type=jnp.float32,
    )


def shift(value, axis, step):
    size = lax.axis_size(axis)
    return lax.ppermute(value, axis, [(i, (i + step) % size) for i in range(size)])


def dispatch_table(routes, gates, expert, capacity):
    rows = routes.shape[0]
    named = routes == expert
    member = jnp.any(named, axis=1).astype(jnp.float32)
    gate = jnp.sum(jnp.where(named, gates, 0.0), axis=1)
    token = lax.broadcasted_iota(jnp.int32, (rows, rows), 0)
    other = lax.broadcasted_iota(jnp.int32, (rows, rows), 1)
    before = jnp.sum(jnp.where(token < other, member[:, None], 0.0), axis=0).astype(jnp.int32)
    slot = lax.broadcasted_iota(jnp.int32, (capacity, rows), 0)
    hit = (slot == before[None, :]) & (member[None, :] > 0)
    slot_gate = jnp.sum(jnp.where(hit, gate[None, :], 0.0), axis=1)
    return hit.astype(jnp.bfloat16), slot_gate


def dispatched(table, slot_gate, pair):
    width = pair.shape[1] // 2
    rows = jnp.dot(table, pair, preferred_element_type=jnp.float32)
    rows_x = rows[:, :width].astype(jnp.bfloat16)
    rows_g = (slot_gate[:, None] * rows[:, width:]).astype(jnp.bfloat16)
    return jnp.concatenate([rows_x, rows_g], axis=1)


def tp_total(part):
    if lax.axis_size("tp") == 2:
        return part.astype(jnp.float32) + shift(part, "tp", 1).astype(jnp.float32)
    share = lax.psum_scatter(part, "tp", scatter_dimension=1, tiled=True)
    return lax.all_gather(share, "tp", axis=1, tiled=True).astype(jnp.float32)


def shards(tokens, cotangent, routes, gates, up_experts, down_experts, up_dense, down_dense):
    tok_rows = tokens.shape[0]
    ep_size = lax.axis_size("ep")
    rep_size = lax.axis_size("rep")
    tp_size = lax.axis_size("tp")
    ep_index = lax.axis_index("ep")
    rep_index = lax.axis_index("rep")
    tp_index = lax.axis_index("tp")
    width = up_experts.shape[1]
    hidden_units = up_experts.shape[2]
    block = hidden_units // rep_size
    capacity = min(tok_rows, 2 * tok_rows // ep_size + tok_rows // 64)
    w_up = up_experts[0]
    w_down = down_experts[0]

    slots = -(-capacity // 8) * 8
    offset = tp_index * width
    pair = jnp.concatenate(
        [
            lax.dynamic_slice_in_dim(tokens, offset, width, 1),
            lax.dynamic_slice_in_dim(cotangent, offset, width, 1),
        ],
        axis=1,
    )
    top_count = routes.shape[1]
    facts = jnp.concatenate([routes.astype(jnp.float32), gates], axis=1)
    facts_of = [shift(facts, "rep", step) if step else facts for step in range(rep_size)]

    def make_pieces(pair, step):
        step_routes = facts_of[step][:, :top_count].astype(jnp.int32)
        step_gates = facts_of[step][:, top_count:]
        tables, pieces = [], []
        for turn in range(ep_size):
            expert = lax.rem(ep_index + turn, ep_size)
            table, slot_gate = dispatch_table(step_routes, step_gates, expert, slots)
            tables.append(table)
            pieces.append(dispatched(table, slot_gate, pair))
        return tables, pieces

    def send(pieces):
        return [shift(piece, "ep", turn) if turn else piece for turn, piece in enumerate(pieces)]

    state = {"w_up": w_up, "w_down": w_down, "down_dense": down_dense}

    def phase_dense_pre():
        state["dense_pre"] = jnp.dot(tokens, up_dense, preferred_element_type=jnp.float32)

    def phase_parts():
        own = jnp.concatenate(arrivals[0], axis=0)
        arrivals[0] = [own]
        state["up_part"] = jnp.dot(
            own[:, :width], state["w_up"], preferred_element_type=jnp.float32
        ).astype(jnp.bfloat16)
        state["down_part"] = contract(own[:, width:], state["w_down"], 1, 1).astype(jnp.bfloat16)
        dense_back = contract(cotangent, state["down_dense"], 1, 1)
        dense_grad_pre = (dense_back * silu_grad(state["dense_pre"])).astype(jnp.bfloat16)
        state["dense_part"] = contract(dense_grad_pre, up_dense, 1, 1).astype(jnp.bfloat16)

    def phase_back():
        hidden = tp_total(state["up_part"])
        grad_hidden = tp_total(state["down_part"])
        state["act"] = jax.nn.silu(hidden).astype(jnp.bfloat16)
        state["pre"] = (grad_hidden * silu_grad(hidden)).astype(jnp.bfloat16)

    work = [phase_dense_pre, phase_parts, phase_back]

    own_tables, pieces = make_pieces(pair, 0)
    arrivals = [send(pieces)]
    for step in range(1, rep_size):
        pair = shift(pair, "rep", 1)
        if step <= len(work):
            work[step - 1]()
            if step == len(work):
                pair, state, arrivals[1] = lax.optimization_barrier((pair, state, arrivals[1]))
            else:
                pair, state = lax.optimization_barrier((pair, state))
        _, pieces = make_pieces(pair, step)
        if 1 < step == rep_size - 1:
            pieces, arrivals[step - 1] = lax.optimization_barrier((pieces, arrivals[step - 1]))
        arrivals.append(send(pieces))
    for item in work[rep_size - 1:]:
        item()

    grad_pre, activation = state["pre"], state["act"]
    dense_part = state["dense_part"]

    row_count = grad_pre.shape[0]

    def exchange(value):
        blocks = value.reshape(row_count, rep_size, block).transpose(1, 0, 2)
        taken = []
        for step in range(rep_size):
            target = lax.rem(rep_index + step, rep_size)
            part = lax.dynamic_index_in_dim(blocks, target, 0, keepdims=False)
            taken.append(shift(part, "rep", step) if step else part)
        return taken

    if tp_size == 2:
        pre_of, act_of = [], []
        for mine in exchange(jnp.where(tp_index == 0, grad_pre, activation)):
            theirs = shift(mine, "tp", 1)
            pre_of.append(jnp.where(tp_index == 0, mine, theirs))
            act_of.append(jnp.where(tp_index == 0, theirs, mine))
    else:
        pre_of, act_of = exchange(grad_pre), exchange(activation)

    route_grad = contract(grad_pre, state["w_up"], 1, 1).astype(jnp.bfloat16)
    returned = []
    for turn in range(ep_size):
        rows = route_grad[turn * slots:(turn + 1) * slots]
        returned.append(shift(rows, "ep", ep_size - turn) if turn else rows)

    replicas = float(rep_size)
    up_total, down_total = 0.0, 0.0
    for step in range(rep_size):
        if step == max(rep_size - 2, 1):
            arrivals[-1], pre_of, act_of, returned, up_total, down_total = (
                lax.optimization_barrier(
                    (arrivals[-1], pre_of, act_of, returned, up_total, down_total)
                )
            )
        rows = jnp.concatenate(arrivals[step], axis=0)
        up_total += contract(rows[:, :width], pre_of[step], 0, 0)
        down_total += contract(act_of[step], rows[:, width:], 0, 0)
    grad_up = (up_total / replicas).astype(jnp.bfloat16)[None]
    grad_down = (down_total / replicas).astype(jnp.bfloat16)[None]

    if tp_size == 2:
        kept = lax.dynamic_slice_in_dim(dense_part, offset, width, 1)
        passed = lax.dynamic_slice_in_dim(dense_part, (1 - tp_index) * width, width, 1)
        dense_grad = kept.astype(jnp.float32) + shift(passed, "tp", 1).astype(jnp.float32)
    else:
        dense_grad = lax.psum_scatter(
            dense_part, "tp", scatter_dimension=1, tiled=True
        ).astype(jnp.float32)

    expert_grad = contract(
        jnp.concatenate(own_tables, axis=0), jnp.concatenate(returned, axis=0), 0, 0
    )
    grad_tokens = (dense_grad + expert_grad).astype(jnp.bfloat16)
    return (grad_tokens, grad_up, grad_down)


def solution(mesh):
    in_specs = (
        P(("rep", "ep"), None),
        P(("rep", "ep"), None),
        P(("rep", "ep"), None),
        P(("rep", "ep"), None),
        P("ep", "tp", None),
        P("ep", None, "tp"),
        P(None, "tp"),
        P("tp", None),
    )
    out_specs = (P(("rep", "ep"), "tp"), P("ep", "tp", "rep"), P("ep", "rep", "tp"))
    return jax.shard_map(shards, mesh=mesh, in_specs=in_specs, out_specs=out_specs, check_vma=False)
```

```python
import jax
import jax.numpy as jnp
from jax import lax
from jax.sharding import PartitionSpec as P


def silu_grad(argument):
    sigmoid_value = jax.nn.sigmoid(argument)
    return sigmoid_value * (1.0 + argument * (1.0 - sigmoid_value))


def contract(left_operand, right_operand, left_axis, right_axis):
    return lax.dot_general(
        left_operand,
        right_operand,
        (((left_axis,), (right_axis,)), ((), ())),
        preferred_element_type=jnp.float32,
    )


def shift(value, axis, step):
    size = lax.axis_size(axis)
    return lax.ppermute(value, axis, [(i, (i + step) % size) for i in range(size)])


def dispatch_table(routes, gates, expert, capacity):
    rows = routes.shape[0]
    named = routes == expert
    member = jnp.any(named, axis=1).astype(jnp.float32)
    gate = jnp.sum(jnp.where(named, gates, 0.0), axis=1)
    token = lax.broadcasted_iota(jnp.int32, (rows, rows), 0)
    other = lax.broadcasted_iota(jnp.int32, (rows, rows), 1)
    before = jnp.sum(jnp.where(token < other, member[:, None], 0.0), axis=0).astype(jnp.int32)
    slot = lax.broadcasted_iota(jnp.int32, (capacity, rows), 0)
    hit = (slot == before[None, :]) & (member[None, :] > 0)
    slot_gate = jnp.sum(jnp.where(hit, gate[None, :], 0.0), axis=1)
    return hit.astype(jnp.bfloat16), slot_gate


def dispatched(table, slot_gate, pair):
    width = pair.shape[1] // 2
    rows = jnp.dot(table, pair, preferred_element_type=jnp.float32)
    rows_x = rows[:, :width].astype(jnp.bfloat16)
    rows_g = (slot_gate[:, None] * rows[:, width:]).astype(jnp.bfloat16)
    return jnp.concatenate([rows_x, rows_g], axis=1)


def tp_total(part):
    if lax.axis_size("tp") == 2:
        return part.astype(jnp.float32) + shift(part, "tp", 1).astype(jnp.float32)
    share = lax.psum_scatter(part, "tp", scatter_dimension=1, tiled=True)
    return lax.all_gather(share, "tp", axis=1, tiled=True).astype(jnp.float32)


def shards(tokens, cotangent, routes, gates, up_experts, down_experts, up_dense, down_dense):
    tok_rows = tokens.shape[0]
    ep_size = lax.axis_size("ep")
    rep_size = lax.axis_size("rep")
    tp_size = lax.axis_size("tp")
    ep_index = lax.axis_index("ep")
    rep_index = lax.axis_index("rep")
    tp_index = lax.axis_index("tp")
    width = up_experts.shape[1]
    hidden_units = up_experts.shape[2]
    block = hidden_units // rep_size
    capacity = min(tok_rows, 2 * tok_rows // ep_size + tok_rows // 64)
    w_up = up_experts[0]
    w_down = down_experts[0]

    slots = -(-capacity // 8) * 8
    offset = tp_index * width
    pair = jnp.concatenate(
        [
            lax.dynamic_slice_in_dim(tokens, offset, width, 1),
            lax.dynamic_slice_in_dim(cotangent, offset, width, 1),
        ],
        axis=1,
    )
    top_count = routes.shape[1]
    facts = jnp.concatenate([routes.astype(jnp.float32), gates], axis=1)
    facts_of = [shift(facts, "rep", step) if step else facts for step in range(rep_size)]

    def make_pieces(pair, step):
        step_routes = facts_of[step][:, :top_count].astype(jnp.int32)
        step_gates = facts_of[step][:, top_count:]
        tables, pieces = [], []
        for turn in range(ep_size):
            expert = lax.rem(ep_index + turn, ep_size)
            table, slot_gate = dispatch_table(step_routes, step_gates, expert, slots)
            tables.append(table)
            pieces.append(dispatched(table, slot_gate, pair))
        return tables, pieces

    def send(pieces):
        return [shift(piece, "ep", turn) if turn else piece for turn, piece in enumerate(pieces)]

    state = {"w_up": w_up, "w_down": w_down, "down_dense": down_dense}

    def phase_dense_pre():
        state["dense_pre"] = jnp.dot(tokens, up_dense, preferred_element_type=jnp.float32)

    def phase_parts():
        own = jnp.concatenate(arrivals[0], axis=0)
        arrivals[0] = [own]
        state["up_part"] = jnp.dot(
            own[:, :width], state["w_up"], preferred_element_type=jnp.float32
        ).astype(jnp.bfloat16)
        state["down_part"] = contract(own[:, width:], state["w_down"], 1, 1).astype(jnp.bfloat16)

    def phase_back():
        hidden = tp_total(state["up_part"])
        grad_hidden = tp_total(state["down_part"])
        state["act"] = jax.nn.silu(hidden).astype(jnp.bfloat16)
        state["pre"] = (grad_hidden * silu_grad(hidden)).astype(jnp.bfloat16)

    work = [phase_dense_pre, phase_parts, phase_back]

    own_tables, pieces = make_pieces(pair, 0)
    arrivals = [send(pieces)]
    for step in range(1, rep_size):
        pair = shift(pair, "rep", 1)
        if step <= len(work):
            work[step - 1]()
            if step == len(work):
                pair, state, arrivals[1] = lax.optimization_barrier((pair, state, arrivals[1]))
            else:
                pair, state = lax.optimization_barrier((pair, state))
        _, pieces = make_pieces(pair, step)
        if 1 < step == rep_size - 1:
            pieces, state, arrivals[step - 1] = lax.optimization_barrier(
                (pieces, state, arrivals[step - 1])
            )
        arrivals.append(send(pieces))
    for item in work[rep_size - 1:]:
        item()

    grad_pre, activation = state["pre"], state["act"]
    dense_back = contract(cotangent, state["down_dense"], 1, 1)
    dense_grad_pre = (dense_back * silu_grad(state["dense_pre"])).astype(jnp.bfloat16)
    dense_part = contract(dense_grad_pre, up_dense, 1, 1).astype(jnp.bfloat16)

    row_count = grad_pre.shape[0]

    def exchange(value):
        blocks = value.reshape(row_count, rep_size, block).transpose(1, 0, 2)
        taken = []
        for step in range(rep_size):
            target = lax.rem(rep_index + step, rep_size)
            part = lax.dynamic_index_in_dim(blocks, target, 0, keepdims=False)
            taken.append(shift(part, "rep", step) if step else part)
        return taken

    if tp_size == 2:
        mine = exchange(jnp.where(tp_index == 0, grad_pre, activation))
        theirs = shift(jnp.stack(mine), "tp", 1)
        pre_of = [jnp.where(tp_index == 0, mine[i], theirs[i]) for i in range(rep_size)]
        act_of = [jnp.where(tp_index == 0, theirs[i], mine[i]) for i in range(rep_size)]
    else:
        pre_of, act_of = exchange(grad_pre), exchange(activation)

    route_grad = contract(grad_pre, state["w_up"], 1, 1).astype(jnp.bfloat16)
    arrivals[-1], pre_of, act_of, dense_part, route_grad = lax.optimization_barrier(
        (arrivals[-1], pre_of, act_of, dense_part, route_grad)
    )
    returned = []
    for turn in range(ep_size):
        rows = route_grad[turn * slots:(turn + 1) * slots]
        returned.append(shift(rows, "ep", ep_size - turn) if turn else rows)

    replicas = float(rep_size)
    up_total, down_total = 0.0, 0.0
    for step in range(rep_size):
        rows = jnp.concatenate(arrivals[step], axis=0)
        up_total += contract(rows[:, :width], pre_of[step], 0, 0)
        down_total += contract(act_of[step], rows[:, width:], 0, 0)
    grad_up = (up_total / replicas).astype(jnp.bfloat16)[None]
    grad_down = (down_total / replicas).astype(jnp.bfloat16)[None]

    if tp_size == 2:
        kept = lax.dynamic_slice_in_dim(dense_part, offset, width, 1)
        passed = lax.dynamic_slice_in_dim(dense_part, (1 - tp_index) * width, width, 1)
        dense_grad = kept.astype(jnp.float32) + shift(passed, "tp", 1).astype(jnp.float32)
    else:
        dense_grad = lax.psum_scatter(
            dense_part, "tp", scatter_dimension=1, tiled=True
        ).astype(jnp.float32)

    expert_grad = contract(
        jnp.concatenate(own_tables, axis=0), jnp.concatenate(returned, axis=0), 0, 0
    )
    grad_tokens = (dense_grad + expert_grad).astype(jnp.bfloat16)
    return (grad_tokens, grad_up, grad_down)


def solution(mesh):
    in_specs = (
        P(("rep", "ep"), None),
        P(("rep", "ep"), None),
        P(("rep", "ep"), None),
        P(("rep", "ep"), None),
        P("ep", "tp", None),
        P("ep", None, "tp"),
        P(None, "tp"),
        P("tp", None),
    )
    out_specs = (P(("rep", "ep"), "tp"), P("ep", "tp", "rep"), P("ep", "rep", "tp"))
    return jax.shard_map(shards, mesh=mesh, in_specs=in_specs, out_specs=out_specs, check_vma=False)
```

```python
import jax
import jax.numpy as jnp
from jax import lax
from jax.sharding import PartitionSpec as P


def silu_grad(argument):
    sigmoid_value = jax.nn.sigmoid(argument)
    return sigmoid_value * (1.0 + argument * (1.0 - sigmoid_value))


def contract(left_operand, right_operand, left_axis, right_axis):
    return lax.dot_general(
        left_operand,
        right_operand,
        (((left_axis,), (right_axis,)), ((), ())),
        preferred_element_type=jnp.float32,
    )


def shift(value, axis, step):
    size = lax.axis_size(axis)
    return lax.ppermute(value, axis, [(i, (i + step) % size) for i in range(size)])


def dispatch_table(routes, gates, expert, capacity):
    rows = routes.shape[0]
    named = routes == expert
    member = jnp.any(named, axis=1).astype(jnp.float32)
    gate = jnp.sum(jnp.where(named, gates, 0.0), axis=1)
    token = lax.broadcasted_iota(jnp.int32, (rows, rows), 0)
    other = lax.broadcasted_iota(jnp.int32, (rows, rows), 1)
    before = jnp.sum(jnp.where(token < other, member[:, None], 0.0), axis=0).astype(jnp.int32)
    slot = lax.broadcasted_iota(jnp.int32, (capacity, rows), 0)
    hit = (slot == before[None, :]) & (member[None, :] > 0)
    slot_gate = jnp.sum(jnp.where(hit, gate[None, :], 0.0), axis=1)
    return hit.astype(jnp.bfloat16), slot_gate


def dispatched(table, slot_gate, pair):
    width = pair.shape[1] // 2
    rows = jnp.dot(table, pair, preferred_element_type=jnp.float32)
    rows_x = rows[:, :width].astype(jnp.bfloat16)
    rows_g = (slot_gate[:, None] * rows[:, width:]).astype(jnp.bfloat16)
    return jnp.concatenate([rows_x, rows_g], axis=1)


def tp_total(part):
    if lax.axis_size("tp") == 2:
        return part.astype(jnp.float32) + shift(part, "tp", 1).astype(jnp.float32)
    share = lax.psum_scatter(part, "tp", scatter_dimension=1, tiled=True)
    return lax.all_gather(share, "tp", axis=1, tiled=True).astype(jnp.float32)


def shards(tokens, cotangent, routes, gates, up_experts, down_experts, up_dense, down_dense):
    tok_rows = tokens.shape[0]
    ep_size = lax.axis_size("ep")
    rep_size = lax.axis_size("rep")
    tp_size = lax.axis_size("tp")
    ep_index = lax.axis_index("ep")
    rep_index = lax.axis_index("rep")
    tp_index = lax.axis_index("tp")
    width = up_experts.shape[1]
    hidden_units = up_experts.shape[2]
    block = hidden_units // rep_size
    capacity = min(tok_rows, 2 * tok_rows // ep_size + tok_rows // 64)
    w_up = up_experts[0]
    w_down = down_experts[0]

    slots = -(-capacity // 8) * 8
    offset = tp_index * width
    pair = jnp.concatenate(
        [
            lax.dynamic_slice_in_dim(tokens, offset, width, 1),
            lax.dynamic_slice_in_dim(cotangent, offset, width, 1),
        ],
        axis=1,
    )
    top_count = routes.shape[1]
    facts = jnp.concatenate([routes.astype(jnp.float32), gates], axis=1)
    facts_of = [shift(facts, "rep", step) if step else facts for step in range(rep_size)]

    def make_pieces(pair, step):
        step_routes = facts_of[step][:, :top_count].astype(jnp.int32)
        step_gates = facts_of[step][:, top_count:]
        tables, pieces = [], []
        for turn in range(ep_size):
            expert = lax.rem(ep_index + turn, ep_size)
            table, slot_gate = dispatch_table(step_routes, step_gates, expert, slots)
            tables.append(table)
            pieces.append(dispatched(table, slot_gate, pair))
        return tables, pieces

    def send(pieces):
        return [shift(piece, "ep", turn) if turn else piece for turn, piece in enumerate(pieces)]

    state = {"w_up": w_up, "w_down": w_down}

    def phase_dense():
        dense_pre = jnp.dot(tokens, up_dense, preferred_element_type=jnp.float32)
        dense_back = contract(cotangent, down_dense, 1, 1)
        state["dense_grad_pre"] = (dense_back * silu_grad(dense_pre)).astype(jnp.bfloat16)

    def phase_parts():
        own = jnp.concatenate(arrivals[0], axis=0)
        arrivals[0] = [own]
        state["up_part"] = jnp.dot(
            own[:, :width], state["w_up"], preferred_element_type=jnp.float32
        ).astype(jnp.bfloat16)
        state["down_part"] = contract(own[:, width:], state["w_down"], 1, 1).astype(jnp.bfloat16)

    def phase_back():
        hidden = tp_total(state["up_part"])
        grad_hidden = tp_total(state["down_part"])
        state["act"] = jax.nn.silu(hidden).astype(jnp.bfloat16)
        state["pre"] = (grad_hidden * silu_grad(hidden)).astype(jnp.bfloat16)

    work = [phase_dense, phase_parts, phase_back]

    own_tables, pieces = make_pieces(pair, 0)
    arrivals = [send(pieces)]
    for step in range(1, rep_size):
        pair = shift(pair, "rep", 1)
        if step <= len(work):
            work[step - 1]()
            if step == len(work):
                pair, state, arrivals[1] = lax.optimization_barrier((pair, state, arrivals[1]))
            else:
                pair, state = lax.optimization_barrier((pair, state))
        _, pieces = make_pieces(pair, step)
        if step == 1:
            pieces, arrivals[0] = lax.optimization_barrier((pieces, arrivals[0]))
        if 1 < step == rep_size - 1:
            pieces, state, arrivals[step - 1] = lax.optimization_barrier(
                (pieces, state, arrivals[step - 1])
            )
        arrivals.append(send(pieces))
    for item in work[rep_size - 1:]:
        item()

    grad_pre, activation = state["pre"], state["act"]
    dense_part = contract(state["dense_grad_pre"], up_dense, 1, 1).astype(jnp.bfloat16)

    row_count = grad_pre.shape[0]

    def exchange(value):
        blocks = value.reshape(row_count, rep_size, block).transpose(1, 0, 2)
        taken = []
        for step in range(rep_size):
            target = lax.rem(rep_index + step, rep_size)
            part = lax.dynamic_index_in_dim(blocks, target, 0, keepdims=False)
            taken.append(shift(part, "rep", step) if step else part)
        return taken

    if tp_size == 2:
        mine = exchange(jnp.where(tp_index == 0, grad_pre, activation))
        theirs = shift(jnp.stack(mine), "tp", 1)
        pre_of = [jnp.where(tp_index == 0, mine[i], theirs[i]) for i in range(rep_size)]
        act_of = [jnp.where(tp_index == 0, theirs[i], mine[i]) for i in range(rep_size)]
    else:
        pre_of, act_of = exchange(grad_pre), exchange(activation)

    route_grad = contract(grad_pre, state["w_up"], 1, 1).astype(jnp.bfloat16)
    arrivals[-1], pre_of, act_of, dense_part, route_grad = lax.optimization_barrier(
        (arrivals[-1], pre_of, act_of, dense_part, route_grad)
    )
    returned = []
    for turn in range(ep_size):
        rows = route_grad[turn * slots:(turn + 1) * slots]
        returned.append(shift(rows, "ep", ep_size - turn) if turn else rows)

    replicas = float(rep_size)
    up_total, down_total = 0.0, 0.0
    for step in range(rep_size):
        rows = jnp.concatenate(arrivals[step], axis=0)
        up_total += contract(rows[:, :width], pre_of[step], 0, 0)
        down_total += contract(act_of[step], rows[:, width:], 0, 0)
    grad_up = (up_total / replicas).astype(jnp.bfloat16)[None]
    grad_down = (down_total / replicas).astype(jnp.bfloat16)[None]

    if tp_size == 2:
        kept = lax.dynamic_slice_in_dim(dense_part, offset, width, 1)
        passed = lax.dynamic_slice_in_dim(dense_part, (1 - tp_index) * width, width, 1)
        dense_grad = kept.astype(jnp.float32) + shift(passed, "tp", 1).astype(jnp.float32)
    else:
        dense_grad = lax.psum_scatter(
            dense_part, "tp", scatter_dimension=1, tiled=True
        ).astype(jnp.float32)

    expert_grad = contract(
        jnp.concatenate(own_tables, axis=0), jnp.concatenate(returned, axis=0), 0, 0
    )
    grad_tokens = (dense_grad + expert_grad).astype(jnp.bfloat16)
    return (grad_tokens, grad_up, grad_down)


def solution(mesh):
    in_specs = (
        P(("rep", "ep"), None),
        P(("rep", "ep"), None),
        P(("rep", "ep"), None),
        P(("rep", "ep"), None),
        P("ep", "tp", None),
        P("ep", None, "tp"),
        P(None, "tp"),
        P("tp", None),
    )
    out_specs = (P(("rep", "ep"), "tp"), P("ep", "tp", "rep"), P("ep", "rep", "tp"))
    return jax.shard_map(shards, mesh=mesh, in_specs=in_specs, out_specs=out_specs, check_vma=False)
```
